32 devices in a mesh: tile: 8 (over z, x), trc: 4 (over y, core).
Axes of the slice: x: 2, y: 2, z: 4, core: 2. Of those that a mesh axis runs over, the one named last changes fastest.
Arguments:
- tracers: float32 [256, 4, 32, 128], P('trc', None, 'tile'), may hold values from 0.1 to 4
- courant_cycle: float32 [4, 32, 128], P(None, 'tile'), may hold values from -0.45 to 0.45
- courant_edge: float32 [4, 32, 128], P(None, 'tile'), may hold values from -0.45 to 0.45
- seam_flags: int32 [8, 2], P('tile'), may hold values from 0 to 1, as said below
- sunlit: int32 [32, 128], P('tile', 'trc'), may hold values from 0 to 1, as said below
- table_entry: int32 [4, 4, 32, 128], P(None, None, 'tile', 'trc'), may hold values from 0 to 3
- linear_maps: bfloat16 [4, 256, 256], replicated, may hold values from -0.375 to 0.375
- offsets: float32 [4, 256], replicated, may hold values from -4 to 4
- mixing: float32 [3, 32, 128], P(None, 'tile', 'trc'), may hold values from 0.05 to 5
Outputs:
- tracers_out: float32 [256, 4, 32, 128], P('trc', None, 'tile')
The draws below stay inside these ranges and needn't reach their ends.
Inputs may be any that keep to these rules, and one draw needn't show every extreme that they name: seam_flags[t, 1] equals seam_flags[t + 1, 0] (tile numbers mod 8); a flag is 1 only on the edge before a tile whose number is a multiple of 2, and at least one flag is 1. In every row of the edge-cell dimension, cycle column x is sunlit exactly when cycle column x + 32 / 2 (mod 32) is not; some tile is sunlit in all of its columns.
All inputs are finite; a program needn't handle non-finite values.
Results may differ from the reference program's by a relative error of at most 0.0025.
Values may be sent and summed in bfloat16 or wider, within the bound.
A program may use at most 64 MiB of HBM per device.

```python
import math
import jax
import jax.numpy as jnp
from jax import lax

SPECIES = 256
LEVELS = 4
EDGE_CELLS = 128
TILE_COLS = 4
SUBSTEPS = 4
ENTRIES = 4
TILES = 8
CYCLE_COLS = 32


def draw_seam_flags(key, part):
    tile_index = jnp.arange(TILES, dtype=jnp.int32)
    face_start = tile_index % (TILES // 4) == 0
    edge_flags = jax.random.randint(jax.random.fold_in(key, 11), (TILES,), 0, 2)
    forced = jax.random.randint(jax.random.fold_in(key, 12), (), 0, 4) * (TILES // 4)
    edge_flags = jnp.where(tile_index == forced, 1, edge_flags)
    edge_flags = jnp.where(face_start, edge_flags, 0).astype(jnp.int32)
    return jnp.stack([edge_flags, jnp.roll(edge_flags, -1)], axis=1)


def draw_sunlit(key, part):
    sun_column = jax.random.randint(jax.random.fold_in(key, 21), (), 0, CYCLE_COLS)
    row_offset = jax.random.randint(jax.random.fold_in(key, 22), (EDGE_CELLS,), 0, TILE_COLS)
    cycle_index = jnp.arange(CYCLE_COLS, dtype=jnp.int32)
    phase = (cycle_index[:, None] - sun_column + row_offset[None, :]) % CYCLE_COLS
    return (phase < CYCLE_COLS // 2).astype(jnp.int32)


def touch_ends(values, own_key, least, high):
    longest = values.shape.index(max(values.shape))
    spots = []
    for shift in (0, 1):
        where = [jax.random.randint(jax.random.fold_in(own_key, axis), (), 0, length) for axis, length in enumerate(values.shape)]
        where[longest] = (where[longest] + shift) % values.shape[longest]
        spots.append(tuple(where))
    return values.at[spots[0]].set(least).at[spots[1]].set(high)


def steps_of(stream_key, dims, shards, smallest, largest):
    def one(dim, blocks):
        heights = jax.random.uniform(jax.random.fold_in(jax.random.fold_in(stream_key, 6), dim), (blocks,), jnp.float32, smallest / len(shards), largest / len(shards))
        return jnp.repeat(jnp.exp(heights), dims[dim] // blocks).reshape((-1,) + (1,) * (len(dims) - dim - 1))

    gain = one(*shards[0])
    for cut in shards[1:]:
        gain = gain * one(*cut)
    return gain


def bell_draw(key, shape, width, limit, kind=jnp.bfloat16):
    array = width * jax.random.normal(key, shape, jnp.float32)
    return jnp.clip(array, min=-limit, max=limit).astype(kind)


def setup_inputs(seed: int = 0) -> dict:
    arg_keys = jax.random.split(jax.random.key(seed), 10)
    return {
        "tracers": jnp.clip(jnp.exp(math.log(4.0) - 3.6888794 * jax.random.uniform(arg_keys[0], (SPECIES, LEVELS, CYCLE_COLS, EDGE_CELLS), jnp.float32) ** steps_of(arg_keys[0], (SPECIES, LEVELS, CYCLE_COLS, EDGE_CELLS), ((0, 4), (2, 8)), -0.2, 0.2)), 0.1, 4.0),
        "courant_cycle": jnp.clip(jax.random.uniform(arg_keys[1], (LEVELS, CYCLE_COLS, EDGE_CELLS), jnp.float32, -0.45, 0.45) * steps_of(arg_keys[1], (LEVELS, CYCLE_COLS, EDGE_CELLS), ((1, 8),), -0.4, 0.0), -0.45, 0.45),
        "courant_edge": jnp.clip(jax.random.uniform(arg_keys[2], (LEVELS, CYCLE_COLS, EDGE_CELLS), jnp.float32, -0.45, 0.45) * steps_of(arg_keys[2], (LEVELS, CYCLE_COLS, EDGE_CELLS), ((1, 8),), -0.4, 0.0), -0.45, 0.45),
        "seam_flags": draw_seam_flags(jax.random.fold_in(arg_keys[9], 71), 0),
        "sunlit": draw_sunlit(jax.random.fold_in(arg_keys[9], 71), 0),
        "table_entry": touch_ends(jax.random.randint(arg_keys[5], (SUBSTEPS, LEVELS, CYCLE_COLS, EDGE_CELLS), 0, ENTRIES), jax.random.fold_in(arg_keys[5], 1), 0, ENTRIES - 1).astype(jnp.int32),
        "linear_maps": bell_draw(arg_keys[6], (ENTRIES, SPECIES, SPECIES), SPECIES ** -0.5, 0.375),
        "offsets": bell_draw(arg_keys[7], (ENTRIES, SPECIES), 0.7, 4.0, jnp.float32),
        "mixing": jnp.clip(jnp.exp(math.log(5.0) - 4.6051702 * jax.random.uniform(arg_keys[8], (LEVELS - 1, CYCLE_COLS, EDGE_CELLS), jnp.float32) ** steps_of(arg_keys[8], (LEVELS - 1, CYCLE_COLS, EDGE_CELLS), ((1, 8), (2, 4)), -0.2, 0.2)), 0.05, 5.0),
    }


def cut_range(values, start, stop, direction):
    return lax.slice_in_dim(values, start, stop, axis=direction)


def edge_values(stencil, direction):
    length = stencil.shape[direction]
    inner_sum = cut_range(stencil, 1, length - 2, direction) + cut_range(stencil, 2, length - 1, direction)
    outer_sum = cut_range(stencil, 0, length - 3, direction) + cut_range(stencil, 3, length, direction)
    return (7.0 / 12.0) * inner_sum - (1.0 / 12.0) * outer_sum


def sweep_flux(stencil, courant, direction):
    inside = stencil.shape[direction] - 6
    edge_vals = edge_values(stencil, direction)
    left_pos = cut_range(edge_vals, 0, inside + 1, direction)
    middle = cut_range(edge_vals, 1, inside + 2, direction)
    right_neg = cut_range(edge_vals, 2, inside + 3, direction)
    center_pos = cut_range(stencil, 2, inside + 3, direction)
    center_neg = cut_range(stencil, 3, inside + 4, direction)
    curve_pos = 6.0 * center_pos - 3.0 * (left_pos + middle)
    flux_pos = courant * (middle - 0.5 * courant * ((middle - left_pos) - (1.0 - 2.0 * courant / 3.0) * curve_pos))
    reverse_speed = -courant
    curve_neg = 6.0 * center_neg - 3.0 * (middle + right_neg)
    flux_neg = courant * (middle + 0.5 * reverse_speed * ((right_neg - middle) + (1.0 - 2.0 * reverse_speed / 3.0) * curve_neg))
    return jnp.where(courant > 0.0, flux_pos, flux_neg)


def tendency(flux, direction):
    length = flux.shape[direction]
    return cut_range(flux, 0, length - 1, direction) - cut_range(flux, 1, length, direction)


def wall_faces(courant_edge):
    closed = jnp.zeros(courant_edge.shape[:-1] + (1,), jnp.float32)
    return jnp.concatenate([closed, courant_edge[..., 1:], closed], axis=-1)


def edge_sweep(tracers, courant_edge):
    stencil = jnp.pad(tracers, ((0, 0), (0, 0), (0, 0), (3, 3)), mode="edge")
    return tendency(sweep_flux(stencil, wall_faces(courant_edge)[None], 3), 3)


def solve_columns(values, coupling):
    levels = values.shape[1]
    zero_row = jnp.zeros(values.shape[2:], jnp.float32)
    ratio_list = []
    solved_list = []
    for level_index in range(levels):
        coupling_below = coupling[level_index - 1] if level_index > 0 else zero_row
        coupling_above = coupling[level_index] if level_index < levels - 1 else zero_row
        diagonal = 1.0 + coupling_below + coupling_above
        if level_index == 0:
            pivot_value = diagonal
            current = values[:, 0] / pivot_value
        else:
            pivot_value = diagonal - coupling_below * ratio_list[-1]
            current = (values[:, level_index] + coupling_below * solved_list[-1]) / pivot_value
        ratio_list.append(coupling_above / pivot_value)
        solved_list.append(current)
    result_list = [solved_list[-1]]
    for level_index in range(levels - 2, -1, -1):
        result_list.append(solved_list[level_index] + ratio_list[level_index] * result_list[-1])
    return jnp.stack(result_list[::-1], axis=1)


def chemistry_steps(rounded, entry_ids, linear_maps, offsets):
    chem_input = rounded
    result = rounded.astype(jnp.float32)
    for substep in range(entry_ids.shape[0]):
        summed = jnp.zeros(rounded.shape, jnp.float32)
        for entry_id in range(linear_maps.shape[0]):
            product = jnp.dot(linear_maps[entry_id].astype(jnp.float32), chem_input.astype(jnp.float32), precision=lax.Precision.HIGHEST)
            summed = jnp.where(entry_ids[substep][None, :] == entry_id, product + offsets[entry_id][:, None], summed)
        result = jnp.maximum(summed, 0.0)
        chem_input = result.astype(jnp.bfloat16)
    return result


def reference(tracers, courant_cycle, courant_edge, seam_flags, sunlit, table_entry, linear_maps, offsets, mixing):
    species, levels, cycle_length, edge_length = tracers.shape
    courant_tiles = courant_cycle.reshape(levels, TILES, TILE_COLS, edge_length)
    next_face = jnp.roll(courant_tiles, -1, axis=1)[:, :, :1, :]
    flip_next = (seam_flags[:, 1] > 0).reshape(1, TILES, 1, 1)
    next_face = jnp.where(flip_next, next_face[..., ::-1], next_face)
    cycle_faces = jnp.concatenate([courant_tiles, next_face], axis=2)
    flip_before = (seam_flags[:, 0] > 0).reshape(1, 1, TILES, 1, 1)
    flip_after = (seam_flags[:, 1] > 0).reshape(1, 1, TILES, 1, 1)

    def advect(group):
        tiled = group.reshape(group.shape[0], levels, TILES, TILE_COLS, edge_length)
        before = jnp.roll(tiled, 1, axis=2)[:, :, :, -3:, :]
        after_cols = jnp.roll(tiled, -1, axis=2)[:, :, :, :3, :]
        before = jnp.where(flip_before, before[..., ::-1], before)
        after_cols = jnp.where(flip_after, after_cols[..., ::-1], after_cols)
        stencil = jnp.concatenate([before, tiled, after_cols], axis=3)
        cycle_part = tendency(sweep_flux(stencil, cycle_faces[None], 3), 3).reshape(group.shape)
        return group + cycle_part + edge_sweep(group, courant_edge)

    group_size = 8
    grouped = tracers.reshape(species // group_size, group_size, levels, cycle_length, edge_length)
    advected = lax.map(advect, grouped).reshape(tracers.shape)
    rounded = advected.astype(jnp.bfloat16)

    conc_tiles = jnp.moveaxis(rounded.reshape(species, levels, TILES, TILE_COLS, edge_length), 2, 0)
    entry_tiles = jnp.moveaxis(table_entry.reshape(table_entry.shape[0], levels, TILES, TILE_COLS, edge_length), 2, 0)
    sun_tiles = sunlit.reshape(TILES, TILE_COLS * edge_length)
    mixing_tiles = jnp.moveaxis(mixing.reshape(levels - 1, TILES, TILE_COLS, edge_length), 1, 0)

    def column_work(pieces):
        conc_tile, entry_tile, sun_tile, mixing_tile = pieces
        columns = TILE_COLS * edge_length
        flat = conc_tile.reshape(species, levels * columns)
        changed = chemistry_steps(flat, entry_tile.reshape(entry_tile.shape[0], levels * columns), linear_maps, offsets)
        daylight = jnp.broadcast_to(sun_tile[None, :] > 0, (levels, columns)).reshape(levels * columns)
        chem_out = jnp.where(daylight[None, :], changed, flat.astype(jnp.float32)).reshape(species, levels, columns)
        return solve_columns(chem_out, mixing_tile.reshape(levels - 1, columns))

    mixed_out = lax.map(column_work, (conc_tiles, entry_tiles, sun_tiles, mixing_tiles))
    mixed_out = mixed_out.reshape(TILES, species, levels, TILE_COLS, edge_length)
    return jnp.moveaxis(mixed_out, 0, 2).reshape(tracers.shape)
```

```python
import functools

import jax
import jax.numpy as jnp
from jax import lax
from jax.experimental import pallas as pl
from jax.experimental.pallas import tpu as pltpu
from jax.sharding import PartitionSpec as P

MESH = pl.DeviceIdType.MESH
WIDTH = 3
CHUNK = 16
f32 = jnp.float32
bf16 = jnp.bfloat16


def block_transpose(parts, lane_block):
    count = len(parts)
    lanes = parts[0].shape[-1]
    step = lanes // count
    parts = list(parts)
    bit = 1
    while bit < count:
        low_half = (lane_block & bit) == 0
        moved = list(parts)
        for i in range(count):
            if i & bit == 0:
                low, high = parts[i], parts[i | bit]
                moved[i] = jnp.where(low_half, low, pltpu.roll(high, step * bit, 1))
                moved[i | bit] = jnp.where(low_half, pltpu.roll(low, lanes - step * bit, 1), high)
        parts = moved
        bit *= 2
    return parts


def flux_weights(u):
    s = jnp.abs(u)
    k = 0.5 * s
    km = k * (1.0 - 2.0 * s / 3.0)
    return u * (1.0 - k - 3.0 * km), u * (k - 3.0 * km), u * (6.0 * km)


def edge_value(a, b, c, d):
    return (7.0 / 12.0) * (b + c) - (1.0 / 12.0) * (a + d)


def kernel(
    dims,
    x_hbm, cc_ref, ce_ref, flag_ref, table_ref, sun_ref, mix_ref, maps_ref, off_ref,
    out_hbm,
    xf, yb, xb, hb, ha, cs, cr, wx, sb, cb, rs, back, mg, offb, coef, mats, load_sem, store_sem,
    halo_send, halo_recv, cour_send, cour_recv, mix_send, mix_recv, fwd_send, fwd_recv, ret_send, ret_recv,
):
    levels, cols, quarter, lanes, tiles, trc, substeps, entries = dims
    me_tile = lax.axis_index("tile")
    me = lax.axis_index("trc")
    after = lax.rem(me_tile + 1, tiles)
    before = lax.rem(me_tile + tiles - 1, tiles)

    loads = []
    for r in range(levels * cols):
        load = pltpu.make_async_copy(x_hbm.at[:, r, 0, :], xf.at[r], load_sem.at[r])
        load.start()
        loads.append(load)

    barrier = pltpu.get_barrier_semaphore()
    for other in (after, before):
        pl.semaphore_signal(barrier, inc=1, device_id={"tile": other, "trc": me}, device_id_type=MESH)
    for d in range(1, trc):
        pl.semaphore_signal(
            barrier, inc=1, device_id={"tile": me_tile, "trc": lax.rem(me + d, trc)}, device_id_type=MESH
        )
    cs[...] = jnp.zeros_like(cs)
    for g in range(levels):
        cs[g : g + 1, :] = cc_ref[g * cols : g * cols + 1, :]
    pl.semaphore_wait(barrier, 2 + trc - 1)

    cour = pltpu.make_async_remote_copy(
        src_ref=cs, dst_ref=cr, send_sem=cour_send, recv_sem=cour_recv,
        device_id={"tile": before, "trc": me}, device_id_type=MESH,
    )
    cour.start()

    halos = []
    for g in range(levels):
        for c in range(cols):
            loads[g * cols + c].wait()
            xb[g, c] = xf[g * cols + c].astype(bf16)
        pair = []
        for way, (other, first, dst) in enumerate(((after, cols - WIDTH, hb), (before, 0, ha))):
            copy = pltpu.make_async_remote_copy(
                src_ref=xb.at[g, pl.ds(first, WIDTH)], dst_ref=dst.at[g],
                send_sem=halo_send.at[way, g], recv_sem=halo_recv.at[way, g],
                device_id={"tile": other, "trc": me}, device_id_type=MESH,
            )
            copy.start()
            pair.append(copy)
        halos.append(pair)
    mixes = []
    for d in range(1, trc):
        copy = pltpu.make_async_remote_copy(
            src_ref=mix_ref, dst_ref=mg.at[me], send_sem=mix_send.at[d - 1], recv_sem=mix_recv.at[d - 1],
            device_id={"tile": me_tile, "trc": lax.rem(me + d, trc)}, device_id_type=MESH,
        )
        copy.start()
        mixes.append(copy)
    mg[me] = mix_ref[...]

    lane = lax.broadcasted_iota(jnp.int32, (CHUNK, lanes), 1)
    lane_block = lane // (lanes // trc)
    u_edge = ce_ref[...]
    row_lane = lax.broadcasted_iota(jnp.int32, u_edge.shape, 1)
    u_edge = jnp.where(row_lane == 0, 0.0, u_edge)
    wa, wb, wc = flux_weights(u_edge)
    wx[0], wx[1], wx[2], wx[3] = wa, wb, wc, u_edge
    chunks = quarter // CHUNK

    def edge_row(r, _):
        a_w = wx[0, pl.ds(r, 1), :]
        b_w = wx[1, pl.ds(r, 1), :]
        c_w = wx[2, pl.ds(r, 1), :]
        up = jnp.broadcast_to(wx[3, pl.ds(r, 1), :], (CHUNK, lanes)) > 0.0
        for i in range(chunks):
            cell = xf[r, pl.ds(i * CHUNK, CHUNK), :]
            m1 = jnp.where(lane < 1, cell, pltpu.roll(cell, 1, 1))
            m2 = jnp.where(lane < 1, cell, pltpu.roll(m1, 1, 1))
            p1 = jnp.where(lane == lanes - 1, cell, pltpu.roll(cell, lanes - 1, 1))
            a = edge_value(m2, m1, cell, p1)
            a_low = pltpu.roll(a, 1, 1)
            last = edge_value(m1, cell, cell, cell)
            a_high = jnp.where(lane == lanes - 1, last, pltpu.roll(a, lanes - 1, 1))
            flux = a_w * a + b_w * jnp.where(up, a_low, a_high) + c_w * jnp.where(up, m1, cell)
            yb[r, pl.ds(i * CHUNK, CHUNK), :] = cell + (flux - pltpu.roll(flux, lanes - 1, 1))
        return 0

    lax.fori_loop(0, levels * cols, edge_row, 0)

    for e in range(entries):
        offb[e] = jnp.broadcast_to(off_ref[:, e : e + 1], offb.shape[1:])
    src = lax.broadcasted_iota(jnp.int32, (lanes, lanes), 0)
    dst = lax.broadcasted_iota(jnp.int32, (lanes, lanes), 1)
    for side in range(2):
        target = jnp.where(flag_ref[0, side] > 0, lanes - 1 - src, src)
        mats[side] = jnp.where(target == dst, 1.0, 0.0)

    cour.wait()
    u_after = jnp.dot(cr[...], mats[1], precision=lax.Precision.HIGHEST, preferred_element_type=f32)
    for g in range(levels):
        coef[3, g] = jnp.zeros(coef.shape[2:], f32)
        coef[3, g, 0:cols, :] = cc_ref[g * cols : (g + 1) * cols, :]
        coef[3, g, cols : cols + 1, :] = u_after[g : g + 1, :]
    wa, wb, wc = flux_weights(coef[3])
    coef[0], coef[1], coef[2] = wa, wb, wc
    rev = [mats[side].astype(bf16) for side in range(2)]

    def cycle_level(g):
        for copy in halos[g]:
            copy.wait_recv()
        ups = [jnp.broadcast_to(coef[3, g, f : f + 1, :], (CHUNK, lanes)) > 0.0 for f in range(cols + 1)]

        def chunk(i, _):
            rows = pl.ds(pl.multiple_of(i * CHUNK, CHUNK), CHUNK)
            cells = [jnp.dot(hb[g, k, rows, :], rev[0], preferred_element_type=f32) for k in range(WIDTH)]
            cells += [xf[g * cols + c, rows, :] for c in range(cols)]
            cells += [jnp.dot(ha[g, k, rows, :], rev[1], preferred_element_type=f32) for k in range(WIDTH)]
            edges = [edge_value(*cells[k : k + 4]) for k in range(cols + 3)]
            fluxes = []
            for f in range(cols + 1):
                far = jnp.where(ups[f], edges[f], edges[f + 2])
                q = jnp.where(ups[f], cells[f + 2], cells[f + 3])
                fluxes.append(
                    coef[0, g, f : f + 1, :] * edges[f + 1]
                    + coef[1, g, f : f + 1, :] * far
                    + coef[2, g, f : f + 1, :] * q
                )
            moved = [yb[g * cols + c, rows, :] + (fluxes[c] - fluxes[c + 1]) for c in range(cols)]
            moved = block_transpose(moved, lane_block)
            for p in range(trc):
                sb[g, p, rows, :] = moved[p].astype(bf16)
            return 0

        lax.fori_loop(0, chunks, chunk, 0)
        sends = []
        for d in range(1, trc):
            peer = lax.rem(me + d, trc)
            copy = pltpu.make_async_remote_copy(
                src_ref=sb.at[g, peer], dst_ref=cb.at[g, me],
                send_sem=fwd_send.at[d - 1, g], recv_sem=fwd_recv.at[d - 1, g],
                device_id={"tile": me_tile, "trc": peer}, device_id_type=MESH,
            )
            copy.start()
            sends.append(copy)
        cb[g, me] = sb[g, me]
        return sends

    species = quarter * trc
    sun = jnp.broadcast_to(sun_ref[...], (species, lanes)) > 0

    def chem_level(g, sends):
        for copy in sends:
            copy.wait_recv()
        conc = cb[g].reshape(species, lanes)
        state = conc
        for s in range(substeps):
            product = jnp.dot(maps_ref[...], state, preferred_element_type=f32)
            entry = jnp.broadcast_to(table_ref[s * levels + g : s * levels + g + 1, :], (species, lanes))
            result = product[:species] + offb[0]
            for e in range(1, entries):
                result = jnp.where(entry == e, product[e * species : (e + 1) * species] + offb[e], result)
            result = jnp.maximum(result, 0.0)
            state = result.astype(bf16)
        chem = jnp.where(sun, result, conc.astype(f32)).astype(bf16)
        rs[g] = chem.reshape(trc, quarter, lanes)
        copies = []
        for d in range(1, trc):
            peer = lax.rem(me + d, trc)
            copy = pltpu.make_async_remote_copy(
                src_ref=rs.at[g, peer], dst_ref=back.at[g, me],
                send_sem=ret_send.at[d - 1, g], recv_sem=ret_recv.at[d - 1, g],
                device_id={"tile": me_tile, "trc": peer}, device_id_type=MESH,
            )
            copy.start()
            copies.append(copy)
        back[g, me] = rs[g, me]
        return copies

    sends = []
    returns = []
    for g in range(levels):
        sends.append(cycle_level(g))
        if g > 0:
            returns.append(chem_level(g - 1, sends[g - 1]))
    returns.append(chem_level(levels - 1, sends[levels - 1]))

    for copy in mixes:
        copy.wait()
    small_block = lax.broadcasted_iota(jnp.int32, mg.shape[1:], 1) // (lanes // trc)
    mixing = block_transpose([mg[q] for q in range(trc)], small_block)
    inverse, below, ratio = [], [], []
    for c in range(cols):
        k = [mixing[c][l : l + 1, :] for l in range(levels - 1)]
        inv_c, rat_c = [], []
        for l in range(levels):
            k_low = k[l - 1] if l > 0 else None
            k_high = k[l] if l < levels - 1 else None
            pivot = 1.0
            if k_low is not None:
                pivot = pivot + k_low - k_low * rat_c[-1]
            if k_high is not None:
                pivot = pivot + k_high
            inv = 1.0 / pivot
            inv_c.append(inv)
            rat_c.append(k_high * inv if k_high is not None else None)
        inverse.append(inv_c)
        ratio.append(rat_c)
        below.append(k)

    for pair in returns:
        for copy in pair:
            copy.wait_recv()

    def solve_chunk(i, _):
        rows = pl.ds(pl.multiple_of(i * CHUNK, CHUNK), CHUNK)
        chem = []
        for g in range(levels):
            chem.append(block_transpose([back[g, q, rows, :].astype(f32) for q in range(trc)], lane_block))
        for c in range(cols):
            solved = []
            for l in range(levels):
                value = chem[l][c]
                if l > 0:
                    value = value + below[c][l - 1] * solved[-1]
                solved.append(value * inverse[c][l])
            current = solved[-1]
            xf[(levels - 1) * cols + c, rows, :] = current
            for l in range(levels - 2, -1, -1):
                current = solved[l] + ratio[c][l] * current
                xf[l * cols + c, rows, :] = current
        return 0

    lax.fori_loop(0, chunks, solve_chunk, 0)
    stores = []
    for r in range(levels * cols):
        store = pltpu.make_async_copy(xf.at[r], out_hbm.at[:, r, 0, :], store_sem.at[r])
        store.start()
        stores.append(store)
    for group in halos + sends + returns:
        for copy in group:
            copy.wait_send()
    for store in stores:
        store.wait()


def shards(
    tiles, trc,
    tracers, courant_cycle, courant_edge, seam_flags, sunlit, table_entry, linear_maps, offsets, mixing,
):
    quarter, levels, cols, lanes = tracers.shape
    substeps = table_entry.shape[0]
    entries, species, _ = linear_maps.shape
    rows = levels * cols
    dims = (levels, cols, quarter, lanes, tiles, trc, substeps, entries)
    vmem = pl.BlockSpec(memory_space=pltpu.VMEM)
    hbm = pl.BlockSpec(memory_space=pl.ANY)
    smem = pl.BlockSpec(memory_space=pltpu.SMEM)
    dma = pltpu.SemaphoreType.DMA
    mix = jnp.pad(mixing.reshape(levels - 1, lanes), ((0, 8 - (levels - 1)), (0, 0)))
    out = pl.pallas_call(
        functools.partial(kernel, dims),
        out_shape=jax.ShapeDtypeStruct((quarter, rows, 1, lanes), f32),
        in_specs=[hbm, vmem, vmem, smem, vmem, vmem, vmem, vmem, vmem],
        out_specs=hbm,
        scratch_shapes=[
            pltpu.VMEM((rows, quarter, lanes), f32),
            pltpu.VMEM((rows, quarter, lanes), f32),
            pltpu.VMEM((levels, cols, quarter, lanes), bf16),
            pltpu.VMEM((levels, WIDTH, quarter, lanes), bf16),
            pltpu.VMEM((levels, WIDTH, quarter, lanes), bf16),
            pltpu.VMEM((8, lanes), f32),
            pltpu.VMEM((8, lanes), f32),
            pltpu.VMEM((4, rows, lanes), f32),
            pltpu.VMEM((levels, trc, quarter, lanes), bf16),
            pltpu.VMEM((levels, trc, quarter, lanes), bf16),
            pltpu.VMEM((levels, trc, quarter, lanes), bf16),
            pltpu.VMEM((levels, trc, quarter, lanes), bf16),
            pltpu.VMEM((trc, 8, lanes), f32),
            pltpu.VMEM((entries, species, lanes), f32),
            pltpu.VMEM((4, levels, 8, lanes), f32),
            pltpu.VMEM((2, lanes, lanes), f32),
            dma((rows,)),
            dma((rows,)),
            dma((2, levels)),
            dma((2, levels)),
            dma,
            dma,
            dma((trc - 1,)),
            dma((trc - 1,)),
            dma((trc - 1, levels)),
            dma((trc - 1, levels)),
            dma((trc - 1, levels)),
            dma((trc - 1, levels)),
        ],
        compiler_params=pltpu.CompilerParams(
            collective_id=0, has_side_effects=True, vmem_limit_bytes=40 * 1024 * 1024
        ),
    )(
        tracers.reshape(quarter, rows, 1, lanes),
        courant_cycle.reshape(rows, lanes),
        courant_edge.reshape(rows, lanes),
        seam_flags,
        table_entry.reshape(substeps * levels, lanes),
        sunlit.reshape(1, lanes),
        mix,
        linear_maps.reshape(entries * species, species),
        offsets.T,
    )
    return out.reshape(tracers.shape)


def solution(mesh):
    placed = (
        P("trc", None, "tile", None),
        P(None, "tile", None),
        P(None, "tile", None),
        P("tile", None),
        P("tile", "trc"),
        P(None, None, "tile", "trc"),
        P(),
        P(),
        P(None, "tile", "trc"),
    )
    return jax.shard_map(
        functools.partial(shards, mesh.shape["tile"], mesh.shape["trc"]),
        mesh=mesh, in_specs=placed, out_specs=P("trc", None, "tile", None), check_vma=False,
    )
```

```python
import functools

import jax
import jax.numpy as jnp
from jax import lax
from jax.experimental import pallas as pl
from jax.experimental.pallas import tpu as pltpu
from jax.sharding import PartitionSpec as P

MESH = pl.DeviceIdType.MESH
WIDTH = 3
CHUNK = 16
f32 = jnp.float32
bf16 = jnp.bfloat16


def block_transpose(parts, lane_block):
    count = len(parts)
    lanes = parts[0].shape[-1]
    step = lanes // count
    parts = list(parts)
    bit = 1
    while bit < count:
        low_half = (lane_block & bit) == 0
        moved = list(parts)
        for i in range(count):
            if i & bit == 0:
                low, high = parts[i], parts[i | bit]
                moved[i] = jnp.where(low_half, low, pltpu.roll(high, step * bit, 1))
                moved[i | bit] = jnp.where(low_half, pltpu.roll(low, lanes - step * bit, 1), high)
        parts = moved
        bit *= 2
    return parts


def flux_weights(u):
    s = jnp.abs(u)
    k = 0.5 * s
    km = k * (1.0 - 2.0 * s / 3.0)
    return u * (1.0 - k - 3.0 * km), u * (k - 3.0 * km), u * (6.0 * km)


def edge_value(a, b, c, d):
    return (7.0 / 12.0) * (b + c) - (1.0 / 12.0) * (a + d)


def kernel(
    dims,
    x_hbm, cc_hbm, ce_hbm, flag_ref, table_hbm, sun_hbm, mix_hbm, maps_hbm, off_hbm,
    out_hbm,
    xf, yb, xb, hb, ha, cs, cr, wx, sb, cb, rs, back, mg, offb, coef, mats,
    cc_ref, ce_ref, tv, sv, mv, maps_ref, off_ref, table_ref, sun_ref, mix_ref, small_sem, load_sem, store_sem,
    halo_send, halo_recv, cour_send, cour_recv, mix_send, mix_recv, fwd_send, fwd_recv, ret_send, ret_recv,
):
    levels, cols, quarter, lanes, tiles, trc, substeps, entries = dims
    me_tile = lax.axis_index("tile")
    me = lax.axis_index("trc")
    after = lax.rem(me_tile + 1, tiles)
    before = lax.rem(me_tile + tiles - 1, tiles)

    first = pltpu.make_async_copy(cc_hbm, cc_ref, small_sem.at[0])
    first.start()
    loads = []
    for r in range(levels * cols):
        load = pltpu.make_async_copy(x_hbm.at[:, r, 0, :], xf.at[r], load_sem.at[r])
        load.start()
        loads.append(load)

    smalls = []
    for i, (source, target) in enumerate(
        ((mix_hbm, mv), (ce_hbm, ce_ref), (off_hbm, off_ref), (sun_hbm, sv), (table_hbm, tv), (maps_hbm, maps_ref))
    ):
        load = pltpu.make_async_copy(source, target, small_sem.at[i + 1])
        load.start()
        smalls.append(load)

    barrier = pltpu.get_barrier_semaphore()
    for other in (after, before):
        pl.semaphore_signal(barrier, inc=1, device_id={"tile": other, "trc": me}, device_id_type=MESH)
    for d in range(1, trc):
        pl.semaphore_signal(
            barrier, inc=1, device_id={"tile": me_tile, "trc": lax.rem(me + d, trc)}, device_id_type=MESH
        )
    first.wait()
    cs[...] = jnp.zeros_like(cs)
    for g in range(levels):
        cs[g : g + 1, :] = cc_ref[g * cols : g * cols + 1, :]
    pl.semaphore_wait(barrier, 2 + trc - 1)

    cour = pltpu.make_async_remote_copy(
        src_ref=cs, dst_ref=cr, send_sem=cour_send, recv_sem=cour_recv,
        device_id={"tile": before, "trc": me}, device_id_type=MESH,
    )
    cour.start()

    halos = []
    for g in range(levels):
        for c in range(cols):
            loads[g * cols + c].wait()
            xb[g, c] = xf[g * cols + c].astype(bf16)
        pair = []
        for way, (other, first, dst) in enumerate(((after, cols - WIDTH, hb), (before, 0, ha))):
            copy = pltpu.make_async_remote_copy(
                src_ref=xb.at[g, pl.ds(first, WIDTH)], dst_ref=dst.at[g],
                send_sem=halo_send.at[way, g], recv_sem=halo_recv.at[way, g],
                device_id={"tile": other, "trc": me}, device_id_type=MESH,
            )
            copy.start()
            pair.append(copy)
        halos.append(pair)
    for load in smalls:
        load.wait()
    mix_ref[...] = jnp.zeros_like(mix_ref)
    mix_ref[0 : levels - 1, :] = jnp.concatenate([mv[:, c, :] for c in range(cols)], axis=1)
    table_ref[...] = jnp.concatenate([tv[:, c, :] for c in range(cols)], axis=1)
    sun_ref[...] = jnp.concatenate([sv[c : c + 1, :] for c in range(cols)], axis=1)
    mixes = []
    for d in range(1, trc):
        copy = pltpu.make_async_remote_copy(
            src_ref=mix_ref, dst_ref=mg.at[me], send_sem=mix_send.at[d - 1], recv_sem=mix_recv.at[d - 1],
            device_id={"tile": me_tile, "trc": lax.rem(me + d, trc)}, device_id_type=MESH,
        )
        copy.start()
        mixes.append(copy)
    mg[me] = mix_ref[...]

    lane = lax.broadcasted_iota(jnp.int32, (CHUNK, lanes), 1)
    lane_block = lane // (lanes // trc)
    u_edge = ce_ref[...]
    row_lane = lax.broadcasted_iota(jnp.int32, u_edge.shape, 1)
    u_edge = jnp.where(row_lane == 0, 0.0, u_edge)
    wa, wb, wc = flux_weights(u_edge)
    wx[0], wx[1], wx[2], wx[3] = wa, wb, wc, u_edge
    chunks = quarter // CHUNK

    def edge_row(r, _):
        a_w = wx[0, pl.ds(r, 1), :]
        b_w = wx[1, pl.ds(r, 1), :]
        c_w = wx[2, pl.ds(r, 1), :]
        up = jnp.broadcast_to(wx[3, pl.ds(r, 1), :], (CHUNK, lanes)) > 0.0
        for i in range(chunks):
            cell = xf[r, pl.ds(i * CHUNK, CHUNK), :]
            m1 = jnp.where(lane < 1, cell, pltpu.roll(cell, 1, 1))
            m2 = jnp.where(lane < 1, cell, pltpu.roll(m1, 1, 1))
            p1 = jnp.where(lane == lanes - 1, cell, pltpu.roll(cell, lanes - 1, 1))
            a = edge_value(m2, m1, cell, p1)
            a_low = pltpu.roll(a, 1, 1)
            last = edge_value(m1, cell, cell, cell)
            a_high = jnp.where(lane == lanes - 1, last, pltpu.roll(a, lanes - 1, 1))
            flux = a_w * a + b_w * jnp.where(up, a_low, a_high) + c_w * jnp.where(up, m1, cell)
            yb[r, pl.ds(i * CHUNK, CHUNK), :] = cell + (flux - pltpu.roll(flux, lanes - 1, 1))
        return 0

    lax.fori_loop(0, levels * cols, edge_row, 0)

    for e in range(entries):
        picked = lax.broadcasted_iota(jnp.int32, (entries, lanes), 0) == e
        offb[e] = lax.dot_general(
            off_ref[...], jnp.where(picked, 1.0, 0.0), (((0,), (0,)), ((), ())),
            precision=lax.Precision.HIGHEST, preferred_element_type=f32,
        )
    src = lax.broadcasted_iota(jnp.int32, (lanes, lanes), 0)
    dst = lax.broadcasted_iota(jnp.int32, (lanes, lanes), 1)
    for side in range(2):
        target = jnp.where(flag_ref[0, side] > 0, lanes - 1 - src, src)
        mats[side] = jnp.where(target == dst, 1.0, 0.0)

    cour.wait()
    u_after = jnp.dot(cr[...], mats[1], precision=lax.Precision.HIGHEST, preferred_element_type=f32)
    for g in range(levels):
        coef[3, g] = jnp.zeros(coef.shape[2:], f32)
        coef[3, g, 0:cols, :] = cc_ref[g * cols : (g + 1) * cols, :]
        coef[3, g, cols : cols + 1, :] = u_after[g : g + 1, :]
    wa, wb, wc = flux_weights(coef[3])
    coef[0], coef[1], coef[2] = wa, wb, wc
    rev = [mats[side].astype(bf16) for side in range(2)]

    def cycle_level(g):
        for copy in halos[g]:
            copy.wait_recv()
        ups = [jnp.broadcast_to(coef[3, g, f : f + 1, :], (CHUNK, lanes)) > 0.0 for f in range(cols + 1)]

        def chunk(i, _):
            rows = pl.ds(pl.multiple_of(i * CHUNK, CHUNK), CHUNK)
            cells = [jnp.dot(hb[g, k, rows, :], rev[0], preferred_element_type=f32) for k in range(WIDTH)]
            cells += [xf[g * cols + c, rows, :] for c in range(cols)]
            cells += [jnp.dot(ha[g, k, rows, :], rev[1], preferred_element_type=f32) for k in range(WIDTH)]
            edges = [edge_value(*cells[k : k + 4]) for k in range(cols + 3)]
            fluxes = []
            for f in range(cols + 1):
                far = jnp.where(ups[f], edges[f], edges[f + 2])
                q = jnp.where(ups[f], cells[f + 2], cells[f + 3])
                fluxes.append(
                    coef[0, g, f : f + 1, :] * edges[f + 1]
                    + coef[1, g, f : f + 1, :] * far
                    + coef[2, g, f : f + 1, :] * q
                )
            moved = [yb[g * cols + c, rows, :] + (fluxes[c] - fluxes[c + 1]) for c in range(cols)]
            moved = block_transpose(moved, lane_block)
            for p in range(trc):
                sb[g, p, rows, :] = moved[p].astype(bf16)
            return 0

        lax.fori_loop(0, chunks, chunk, 0)
        sends = []
        for d in range(1, trc):
            peer = lax.rem(me + d, trc)
            copy = pltpu.make_async_remote_copy(
                src_ref=sb.at[g, peer], dst_ref=cb.at[g, me],
                send_sem=fwd_send.at[d - 1, g], recv_sem=fwd_recv.at[d - 1, g],
                device_id={"tile": me_tile, "trc": peer}, device_id_type=MESH,
            )
            copy.start()
            sends.append(copy)
        cb[g, me] = sb[g, me]
        return sends

    species = quarter * trc
    sun = jnp.broadcast_to(sun_ref[...], (species, lanes)) > 0

    def chem_level(g, sends):
        for copy in sends:
            copy.wait_recv()
        conc = cb[g].reshape(species, lanes)
        state = conc
        for s in range(substeps):
            product = jnp.dot(maps_ref[...], state, preferred_element_type=f32)
            entry = jnp.broadcast_to(table_ref[s * levels + g : s * levels + g + 1, :], (species, lanes))
            result = product[:species] + offb[0]
            for e in range(1, entries):
                result = jnp.where(entry == e, product[e * species : (e + 1) * species] + offb[e], result)
            result = jnp.maximum(result, 0.0)
            state = result.astype(bf16)
        chem = jnp.where(sun, result, conc.astype(f32)).astype(bf16)
        rs[g] = chem.reshape(trc, quarter, lanes)
        copies = []
        for d in range(1, trc):
            peer = lax.rem(me + d, trc)
            copy = pltpu.make_async_remote_copy(
                src_ref=rs.at[g, peer], dst_ref=back.at[g, me],
                send_sem=ret_send.at[d - 1, g], recv_sem=ret_recv.at[d - 1, g],
                device_id={"tile": me_tile, "trc": peer}, device_id_type=MESH,
            )
            copy.start()
            copies.append(copy)
        back[g, me] = rs[g, me]
        return copies

    sends = []
    returns = []
    for g in range(levels):
        sends.append(cycle_level(g))
        if g > 0:
            returns.append(chem_level(g - 1, sends[g - 1]))
    returns.append(chem_level(levels - 1, sends[levels - 1]))

    for copy in mixes:
        copy.wait()
    small_block = lax.broadcasted_iota(jnp.int32, mg.shape[1:], 1) // (lanes // trc)
    mixing = block_transpose([mg[q] for q in range(trc)], small_block)
    inverse, below, ratio = [], [], []
    for c in range(cols):
        k = [mixing[c][l : l + 1, :] for l in range(levels - 1)]
        inv_c, rat_c = [], []
        for l in range(levels):
            k_low = k[l - 1] if l > 0 else None
            k_high = k[l] if l < levels - 1 else None
            pivot = 1.0
            if k_low is not None:
                pivot = pivot + k_low - k_low * rat_c[-1]
            if k_high is not None:
                pivot = pivot + k_high
            inv = 1.0 / pivot
            inv_c.append(inv)
            rat_c.append(k_high * inv if k_high is not None else None)
        inverse.append(inv_c)
        ratio.append(rat_c)
        below.append(k)

    for pair in returns:
        for copy in pair:
            copy.wait_recv()

    def solve_chunk(i, _):
        rows = pl.ds(pl.multiple_of(i * CHUNK, CHUNK), CHUNK)
        chem = []
        for g in range(levels):
            chem.append(block_transpose([back[g, q, rows, :].astype(f32) for q in range(trc)], lane_block))
        for c in range(cols):
            solved = []
            for l in range(levels):
                value = chem[l][c]
                if l > 0:
                    value = value + below[c][l - 1] * solved[-1]
                solved.append(value * inverse[c][l])
            current = solved[-1]
            xf[(levels - 1) * cols + c, rows, :] = current
            for l in range(levels - 2, -1, -1):
                current = solved[l] + ratio[c][l] * current
                xf[l * cols + c, rows, :] = current
        return 0

    lax.fori_loop(0, chunks, solve_chunk, 0)
    stores = []
    for r in range(levels * cols):
        store = pltpu.make_async_copy(xf.at[r], out_hbm.at[:, r, 0, :], store_sem.at[r])
        store.start()
        stores.append(store)
    for group in halos + sends + returns:
        for copy in group:
            copy.wait_send()
    for store in stores:
        store.wait()


def shards(
    tiles, trc,
    tracers, courant_cycle, courant_edge, seam_flags, sunlit, table_entry, linear_maps, offsets, mixing,
):
    quarter, levels, cols, lanes = tracers.shape
    substeps = table_entry.shape[0]
    entries, species, _ = linear_maps.shape
    rows = levels * cols
    dims = (levels, cols, quarter, lanes, tiles, trc, substeps, entries)
    hbm = pl.BlockSpec(memory_space=pl.ANY)
    smem = pl.BlockSpec(memory_space=pltpu.SMEM)
    dma = pltpu.SemaphoreType.DMA
    out = pl.pallas_call(
        functools.partial(kernel, dims),
        out_shape=jax.ShapeDtypeStruct((quarter, rows, 1, lanes), f32),
        in_specs=[hbm, hbm, hbm, smem, hbm, hbm, hbm, hbm, hbm],
        out_specs=hbm,
        scratch_shapes=[
            pltpu.VMEM((rows, quarter, lanes), f32),
            pltpu.VMEM((rows, quarter, lanes), f32),
            pltpu.VMEM((levels, cols, quarter, lanes), bf16),
            pltpu.VMEM((levels, WIDTH, quarter, lanes), bf16),
            pltpu.VMEM((levels, WIDTH, quarter, lanes), bf16),
            pltpu.VMEM((8, lanes), f32),
            pltpu.VMEM((8, lanes), f32),
            pltpu.VMEM((4, rows, lanes), f32),
            pltpu.VMEM((levels, trc, quarter, lanes), bf16),
            pltpu.VMEM((levels, trc, quarter, lanes), bf16),
            pltpu.VMEM((levels, trc, quarter, lanes), bf16),
            pltpu.VMEM((levels, trc, quarter, lanes), bf16),
            pltpu.VMEM((trc, 8, lanes), f32),
            pltpu.VMEM((entries, species, lanes), f32),
            pltpu.VMEM((4, levels, 8, lanes), f32),
            pltpu.VMEM((2, lanes, lanes), f32),
            pltpu.VMEM((rows, lanes), f32),
            pltpu.VMEM((rows, lanes), f32),
            pltpu.VMEM((substeps * levels, cols, lanes // trc), jnp.int32),
            pltpu.VMEM((cols, lanes // trc), jnp.int32),
            pltpu.VMEM((levels - 1, cols, lanes // trc), f32),
            pltpu.VMEM((entries * species, species), bf16),
            pltpu.VMEM((entries, species), f32),
            pltpu.VMEM((substeps * levels, lanes), jnp.int32),
            pltpu.VMEM((1, lanes), jnp.int32),
            pltpu.VMEM((8, lanes), f32),
            dma((7,)),
            dma((rows,)),
            dma((rows,)),
            dma((2, levels)),
            dma((2, levels)),
            dma,
            dma,
            dma((trc - 1,)),
            dma((trc - 1,)),
            dma((trc - 1, levels)),
            dma((trc - 1, levels)),
            dma((trc - 1, levels)),
            dma((trc - 1, levels)),
        ],
        compiler_params=pltpu.CompilerParams(
            collective_id=0, has_side_effects=True, vmem_limit_bytes=60 * 1024 * 1024
        ),
    )(
        tracers.reshape(quarter, rows, 1, lanes),
        courant_cycle.reshape(rows, lanes),
        courant_edge.reshape(rows, lanes),
        seam_flags,
        table_entry.reshape(substeps * levels, cols, lanes // trc),
        sunlit,
        mixing,
        linear_maps.reshape(entries * species, species),
        offsets,
    )
    return out.reshape(tracers.shape)


def solution(mesh):
    placed = (
        P("trc", None, "tile", None),
        P(None, "tile", None),
        P(None, "tile", None),
        P("tile", None),
        P("tile", "trc"),
        P(None, None, "tile", "trc"),
        P(),
        P(),
        P(None, "tile", "trc"),
    )
    return jax.shard_map(
        functools.partial(shards, mesh.shape["tile"], mesh.shape["trc"]),
        mesh=mesh, in_specs=placed, out_specs=P("trc", None, "tile", None), check_vma=False,
    )
```

```python
import functools

import jax
import jax.numpy as jnp
from jax import lax
from jax.experimental import pallas as pl
from jax.experimental.pallas import tpu as pltpu
from jax.sharding import PartitionSpec as P

MESH = pl.DeviceIdType.MESH
WIDTH = 3
CHUNK = 16
f32 = jnp.float32
bf16 = jnp.bfloat16


def block_transpose(parts, lane_block):
    count = len(parts)
    lanes = parts[0].shape[-1]
    step = lanes // count
    parts = list(parts)
    bit = 1
    while bit < count:
        low_half = (lane_block & bit) == 0
        moved = list(parts)
        for i in range(count):
            if i & bit == 0:
                low, high = parts[i], parts[i | bit]
                moved[i] = jnp.where(low_half, low, pltpu.roll(high, step * bit, 1))
                moved[i | bit] = jnp.where(low_half, pltpu.roll(low, lanes - step * bit, 1), high)
        parts = moved
        bit *= 2
    return parts


def flux_weights(u):
    s = jnp.abs(u)
    k = 0.5 * s
    km = k * (1.0 - 2.0 * s / 3.0)
    return u * (1.0 - k - 3.0 * km), u * (k - 3.0 * km), u * (6.0 * km)


def edge_value(a, b, c, d):
    return (7.0 / 12.0) * (b + c) - (1.0 / 12.0) * (a + d)


def kernel(
    dims,
    x_hbm, cc_hbm, ce_hbm, flag_ref, table_hbm, sun_hbm, mix_hbm, maps_hbm, off_hbm,
    out_hbm,
    xf, yb, xb, hb, ha, cs, cr, wx, sb, cb, rs, back, mg, offb, coef, mats, hf,
    cc_ref, ce_ref, tv, sv, mv, maps_ref, off_ref, table_ref, sun_ref, mix_ref, small_sem, load_sem, store_sem,
    halo_send, halo_recv, cour_send, cour_recv, mix_send, mix_recv, fwd_send, fwd_recv, ret_send, ret_recv,
):
    levels, cols, quarter, lanes, tiles, trc, substeps, entries = dims
    me_tile = lax.axis_index("tile")
    me = lax.axis_index("trc")
    after = lax.rem(me_tile + 1, tiles)
    before = lax.rem(me_tile + tiles - 1, tiles)

    first = pltpu.make_async_copy(cc_hbm, cc_ref, small_sem.at[0])
    first.start()
    loads = []
    for r in range(levels * cols):
        load = pltpu.make_async_copy(x_hbm.at[:, r, 0, :], xf.at[r], load_sem.at[r])
        load.start()
        loads.append(load)

    smalls = []
    for i, (source, target) in enumerate(
        ((mix_hbm, mv), (ce_hbm, ce_ref), (off_hbm, off_ref), (sun_hbm, sv), (table_hbm, tv), (maps_hbm, maps_ref))
    ):
        load = pltpu.make_async_copy(source, target, small_sem.at[i + 1])
        load.start()
        smalls.append(load)

    barrier = pltpu.get_barrier_semaphore()
    for other in (after, before):
        pl.semaphore_signal(barrier, inc=1, device_id={"tile": other, "trc": me}, device_id_type=MESH)
    for d in range(1, trc):
        pl.semaphore_signal(
            barrier, inc=1, device_id={"tile": me_tile, "trc": lax.rem(me + d, trc)}, device_id_type=MESH
        )
    first.wait()
    cs[...] = jnp.zeros_like(cs)
    for g in range(levels):
        cs[g : g + 1, :] = cc_ref[g * cols : g * cols + 1, :]
    pl.semaphore_wait(barrier, 2 + trc - 1)

    cour = pltpu.make_async_remote_copy(
        src_ref=cs, dst_ref=cr, send_sem=cour_send, recv_sem=cour_recv,
        device_id={"tile": before, "trc": me}, device_id_type=MESH,
    )
    cour.start()

    halos = []
    for g in range(levels):
        for c in range(cols):
            loads[g * cols + c].wait()
            xb[g, c] = xf[g * cols + c].astype(bf16)
        pair = []
        for way, (other, first, dst) in enumerate(((after, cols - WIDTH, hb), (before, 0, ha))):
            copy = pltpu.make_async_remote_copy(
                src_ref=xb.at[g, pl.ds(first, WIDTH)], dst_ref=dst.at[g],
                send_sem=halo_send.at[way, g], recv_sem=halo_recv.at[way, g],
                device_id={"tile": other, "trc": me}, device_id_type=MESH,
            )
            copy.start()
            pair.append(copy)
        halos.append(pair)
    for load in smalls:
        load.wait()
    mix_ref[...] = jnp.zeros_like(mix_ref)
    mix_ref[0 : levels - 1, :] = jnp.concatenate([mv[:, c, :] for c in range(cols)], axis=1)
    table_ref[...] = jnp.concatenate([tv[:, c, :] for c in range(cols)], axis=1)
    sun_ref[...] = jnp.concatenate([sv[c : c + 1, :] for c in range(cols)], axis=1)
    mixes = []
    for d in range(1, trc):
        copy = pltpu.make_async_remote_copy(
            src_ref=mix_ref, dst_ref=mg.at[me], send_sem=mix_send.at[d - 1], recv_sem=mix_recv.at[d - 1],
            device_id={"tile": me_tile, "trc": lax.rem(me + d, trc)}, device_id_type=MESH,
        )
        copy.start()
        mixes.append(copy)
    mg[me] = mix_ref[...]

    lane = lax.broadcasted_iota(jnp.int32, (CHUNK, lanes), 1)
    lane_block = lane // (lanes // trc)
    u_edge = ce_ref[...]
    row_lane = lax.broadcasted_iota(jnp.int32, u_edge.shape, 1)
    u_edge = jnp.where(row_lane == 0, 0.0, u_edge)
    wa, wb, wc = flux_weights(u_edge)
    wx[0], wx[1], wx[2], wx[3] = wa, wb, wc, u_edge
    chunks = quarter // CHUNK

    def edge_row(r, _):
        a_w = wx[0, pl.ds(r, 1), :]
        b_w = wx[1, pl.ds(r, 1), :]
        c_w = wx[2, pl.ds(r, 1), :]
        up = jnp.broadcast_to(wx[3, pl.ds(r, 1), :], (CHUNK, lanes)) > 0.0
        for i in range(chunks):
            cell = xf[r, pl.ds(i * CHUNK, CHUNK), :]
            m1 = jnp.where(lane < 1, cell, pltpu.roll(cell, 1, 1))
            m2 = jnp.where(lane < 2, m1, pltpu.roll(cell, 2, 1))
            m3 = jnp.where(lane < 3, m2, pltpu.roll(cell, 3, 1))
            p1 = jnp.where(lane == lanes - 1, cell, pltpu.roll(cell, lanes - 1, 1))
            p2 = jnp.where(lane >= lanes - 2, p1, pltpu.roll(cell, lanes - 2, 1))
            near = edge_value(m2, m1, cell, p1)
            far = edge_value(
                jnp.where(up, m3, m1), jnp.where(up, m2, cell), jnp.where(up, m1, p1), jnp.where(up, cell, p2)
            )
            flux = a_w * near + b_w * far + c_w * jnp.where(up, m1, cell)
            yb[r, pl.ds(i * CHUNK, CHUNK), :] = cell + (flux - pltpu.roll(flux, lanes - 1, 1))
        return 0

    lax.fori_loop(0, levels * cols, edge_row, 0, unroll=2)

    for e in range(entries):
        picked = lax.broadcasted_iota(jnp.int32, (entries, lanes), 0) == e
        offb[e] = lax.dot_general(
            off_ref[...], jnp.where(picked, 1.0, 0.0), (((0,), (0,)), ((), ())),
            precision=lax.Precision.HIGHEST, preferred_element_type=f32,
        )
    src = lax.broadcasted_iota(jnp.int32, (lanes, lanes), 0)
    dst = lax.broadcasted_iota(jnp.int32, (lanes, lanes), 1)
    for side in range(2):
        target = jnp.where(flag_ref[0, side] > 0, lanes - 1 - src, src)
        mats[side] = jnp.where(target == dst, 1.0, 0.0)

    cour.wait()
    u_after = jnp.dot(cr[...], mats[1], precision=lax.Precision.HIGHEST, preferred_element_type=f32)
    for g in range(levels):
        coef[3, g] = jnp.zeros(coef.shape[2:], f32)
        coef[3, g, 0:cols, :] = cc_ref[g * cols : (g + 1) * cols, :]
        coef[3, g, cols : cols + 1, :] = u_after[g : g + 1, :]
    wa, wb, wc = flux_weights(coef[3])
    coef[0], coef[1], coef[2] = wa, wb, wc
    rev = [mats[side].astype(bf16) for side in range(2)]

    def cycle_level(g):
        for copy in halos[g]:
            copy.wait_recv()
        for side, halo in enumerate((hb, ha)):
            turned = jnp.dot(halo[g].reshape(WIDTH * quarter, lanes), rev[side], preferred_element_type=f32)
            hf[side] = turned.reshape(WIDTH, quarter, lanes)
        ups = [jnp.broadcast_to(coef[3, g, f : f + 1, :], (CHUNK, lanes)) > 0.0 for f in range(cols + 1)]

        def chunk(i, _):
            rows = pl.ds(pl.multiple_of(i * CHUNK, CHUNK), CHUNK)
            cells = [hf[0, k, rows, :] for k in range(WIDTH)]
            cells += [xf[g * cols + c, rows, :] for c in range(cols)]
            cells += [hf[1, k, rows, :] for k in range(WIDTH)]
            edges = [edge_value(*cells[k : k + 4]) for k in range(cols + 3)]
            fluxes = []
            for f in range(cols + 1):
                far = jnp.where(ups[f], edges[f], edges[f + 2])
                q = jnp.where(ups[f], cells[f + 2], cells[f + 3])
                fluxes.append(
                    coef[0, g, f : f + 1, :] * edges[f + 1]
                    + coef[1, g, f : f + 1, :] * far
                    + coef[2, g, f : f + 1, :] * q
                )
            moved = [yb[g * cols + c, rows, :] + (fluxes[c] - fluxes[c + 1]) for c in range(cols)]
            moved = block_transpose(moved, lane_block)
            for p in range(trc):
                sb[g, p, rows, :] = moved[p].astype(bf16)
            return 0

        lax.fori_loop(0, chunks, chunk, 0, unroll=2)
        sends = []
        for d in range(1, trc):
            peer = lax.rem(me + d, trc)
            copy = pltpu.make_async_remote_copy(
                src_ref=sb.at[g, peer], dst_ref=cb.at[g, me],
                send_sem=fwd_send.at[d - 1, g], recv_sem=fwd_recv.at[d - 1, g],
                device_id={"tile": me_tile, "trc": peer}, device_id_type=MESH,
            )
            copy.start()
            sends.append(copy)
        cb[g, me] = sb[g, me]
        return sends

    species = quarter * trc
    sun = jnp.broadcast_to(sun_ref[...], (species, lanes)) > 0

    def chem_levels(group):
        for g in group:
            for copy in sends[g]:
                copy.wait_recv()
        conc = [cb[g].reshape(species, lanes) for g in group]
        states = conc
        for s in range(substeps):
            product = jnp.dot(maps_ref[...], jnp.concatenate(states, axis=1), preferred_element_type=f32)
            results = []
            for i, g in enumerate(group):
                row = s * levels + g
                entry = jnp.broadcast_to(table_ref[row : row + 1, :], (species, lanes))
                part = product[:, i * lanes : (i + 1) * lanes]
                result = part[:species] + offb[0]
                for e in range(1, entries):
                    result = jnp.where(entry == e, part[e * species : (e + 1) * species] + offb[e], result)
                results.append(jnp.maximum(result, 0.0))
            states = [result.astype(bf16) for result in results]
        copies = []
        for i, g in enumerate(group):
            chem = jnp.where(sun, results[i], conc[i].astype(f32)).astype(bf16)
            rs[g] = chem.reshape(trc, quarter, lanes)
            for d in range(1, trc):
                peer = lax.rem(me + d, trc)
                copy = pltpu.make_async_remote_copy(
                    src_ref=rs.at[g, peer], dst_ref=back.at[g, me],
                    send_sem=ret_send.at[d - 1, g], recv_sem=ret_recv.at[d - 1, g],
                    device_id={"tile": me_tile, "trc": peer}, device_id_type=MESH,
                )
                copy.start()
                copies.append(copy)
            back[g, me] = rs[g, me]
        return copies

    sends = [cycle_level(g) for g in range(levels)]
    returns = [chem_levels(range(g, min(g + 2, levels))) for g in range(0, levels, 2)]

    for copy in mixes:
        copy.wait()
    small_block = lax.broadcasted_iota(jnp.int32, mg.shape[1:], 1) // (lanes // trc)
    mixing = block_transpose([mg[q] for q in range(trc)], small_block)
    inverse, below, ratio = [], [], []
    for c in range(cols):
        k = [mixing[c][l : l + 1, :] for l in range(levels - 1)]
        inv_c, rat_c = [], []
        for l in range(levels):
            k_low = k[l - 1] if l > 0 else None
            k_high = k[l] if l < levels - 1 else None
            pivot = 1.0
            if k_low is not None:
                pivot = pivot + k_low - k_low * rat_c[-1]
            if k_high is not None:
                pivot = pivot + k_high
            inv = 1.0 / pivot
            inv_c.append(inv)
            rat_c.append(k_high * inv if k_high is not None else None)
        inverse.append(inv_c)
        ratio.append(rat_c)
        below.append(k)

    for pair in returns:
        for copy in pair:
            copy.wait_recv()

    def solve_chunk(i, _):
        rows = pl.ds(pl.multiple_of(i * CHUNK, CHUNK), CHUNK)
        chem = []
        for g in range(levels):
            chem.append(block_transpose([back[g, q, rows, :].astype(f32) for q in range(trc)], lane_block))
        for c in range(cols):
            solved = []
            for l in range(levels):
                value = chem[l][c]
                if l > 0:
                    value = value + below[c][l - 1] * solved[-1]
                solved.append(value * inverse[c][l])
            current = solved[-1]
            xf[(levels - 1) * cols + c, rows, :] = current
            for l in range(levels - 2, -1, -1):
                current = solved[l] + ratio[c][l] * current
                xf[l * cols + c, rows, :] = current
        return 0

    lax.fori_loop(0, chunks, solve_chunk, 0, unroll=2)
    stores = []
    for r in range(levels * cols):
        store = pltpu.make_async_copy(xf.at[r], out_hbm.at[:, r, 0, :], store_sem.at[r])
        store.start()
        stores.append(store)
    for group in halos + sends + returns:
        for copy in group:
            copy.wait_send()
    for store in stores:
        store.wait()


def shards(
    tiles, trc,
    tracers, courant_cycle, courant_edge, seam_flags, sunlit, table_entry, linear_maps, offsets, mixing,
):
    quarter, levels, cols, lanes = tracers.shape
    substeps = table_entry.shape[0]
    entries, species, _ = linear_maps.shape
    rows = levels * cols
    dims = (levels, cols, quarter, lanes, tiles, trc, substeps, entries)
    hbm = pl.BlockSpec(memory_space=pl.ANY)
    smem = pl.BlockSpec(memory_space=pltpu.SMEM)
    dma = pltpu.SemaphoreType.DMA
    out = pl.pallas_call(
        functools.partial(kernel, dims),
        out_shape=jax.ShapeDtypeStruct((quarter, rows, 1, lanes), f32),
        in_specs=[hbm, hbm, hbm, smem, hbm, hbm, hbm, hbm, hbm],
        out_specs=hbm,
        scratch_shapes=[
            pltpu.VMEM((rows, quarter, lanes), f32),
            pltpu.VMEM((rows, quarter, lanes), f32),
            pltpu.VMEM((levels, cols, quarter, lanes), bf16),
            pltpu.VMEM((levels, WIDTH, quarter, lanes), bf16),
            pltpu.VMEM((levels, WIDTH, quarter, lanes), bf16),
            pltpu.VMEM((8, lanes), f32),
            pltpu.VMEM((8, lanes), f32),
            pltpu.VMEM((4, rows, lanes), f32),
            pltpu.VMEM((levels, trc, quarter, lanes), bf16),
            pltpu.VMEM((levels, trc, quarter, lanes), bf16),
            pltpu.VMEM((levels, trc, quarter, lanes), bf16),
            pltpu.VMEM((levels, trc, quarter, lanes), bf16),
            pltpu.VMEM((trc, 8, lanes), f32),
            pltpu.VMEM((entries, species, lanes), f32),
            pltpu.VMEM((4, levels, 8, lanes), f32),
            pltpu.VMEM((2, lanes, lanes), f32),
            pltpu.VMEM((2, WIDTH, quarter, lanes), f32),
            pltpu.VMEM((rows, lanes), f32),
            pltpu.VMEM((rows, lanes), f32),
            pltpu.VMEM((substeps * levels, cols, lanes // trc), jnp.int32),
            pltpu.VMEM((cols, lanes // trc), jnp.int32),
            pltpu.VMEM((levels - 1, cols, lanes // trc), f32),
            pltpu.VMEM((entries * species, species), bf16),
            pltpu.VMEM((entries, species), f32),
            pltpu.VMEM((substeps * levels, lanes), jnp.int32),
            pltpu.VMEM((1, lanes), jnp.int32),
            pltpu.VMEM((8, lanes), f32),
            dma((7,)),
            dma((rows,)),
            dma((rows,)),
            dma((2, levels)),
            dma((2, levels)),
            dma,
            dma,
            dma((trc - 1,)),
            dma((trc - 1,)),
            dma((trc - 1, levels)),
            dma((trc - 1, levels)),
            dma((trc - 1, levels)),
            dma((trc - 1, levels)),
        ],
        compiler_params=pltpu.CompilerParams(
            collective_id=0, has_side_effects=True, vmem_limit_bytes=60 * 1024 * 1024
        ),
    )(
        tracers.reshape(quarter, rows, 1, lanes),
        courant_cycle.reshape(rows, lanes),
        courant_edge.reshape(rows, lanes),
        seam_flags,
        table_entry.reshape(substeps * levels, cols, lanes // trc),
        sunlit,
        mixing,
        linear_maps.reshape(entries * species, species),
        offsets,
    )
    return out.reshape(tracers.shape)


def solution(mesh):
    placed = (
        P("trc", None, "tile", None),
        P(None, "tile", None),
        P(None, "tile", None),
        P("tile", None),
        P("tile", "trc"),
        P(None, None, "tile", "trc"),
        P(),
        P(),
        P(None, "tile", "trc"),
    )
    return jax.shard_map(
        functools.partial(shards, mesh.shape["tile"], mesh.shape["trc"]),
        mesh=mesh, in_specs=placed, out_specs=P("trc", None, "tile", None), check_vma=False,
    )
```

```python
import functools

import jax
import jax.numpy as jnp
from jax import lax
from jax.experimental import pallas as pl
from jax.experimental.pallas import tpu as pltpu
from jax.sharding import PartitionSpec as P

MESH = pl.DeviceIdType.MESH
WIDTH = 3
CHUNK = 16
f32 = jnp.float32
bf16 = jnp.bfloat16


def block_transpose(parts, lane_block):
    count = len(parts)
    lanes = parts[0].shape[-1]
    step = lanes // count
    parts = list(parts)
    bit = 1
    while bit < count:
        low_half = (lane_block & bit) == 0
        moved = list(parts)
        for i in range(count):
            if i & bit == 0:
                low, high = parts[i], parts[i | bit]
                moved[i] = jnp.where(low_half, low, pltpu.roll(high, step * bit, 1))
                moved[i | bit] = jnp.where(low_half, pltpu.roll(low, lanes - step * bit, 1), high)
        parts = moved
        bit *= 2
    return parts


def flux_weights(u):
    s = jnp.abs(u)
    k = 0.5 * s
    km = k * (1.0 - 2.0 * s / 3.0)
    return u * (1.0 - k - 3.0 * km), u * (k - 3.0 * km), u * (6.0 * km)


def edge_value(a, b, c, d):
    return (7.0 / 12.0) * (b + c) - (1.0 / 12.0) * (a + d)


def kernel(
    dims,
    x_hbm, cc_hbm, ce_hbm, flag_ref, table_hbm, sun_hbm, mix_hbm, maps_hbm, off_hbm,
    out_hbm,
    xf, yb, xb, hb, ha, cs, cr, wx, sb, cb, rs, back, mg, offb, coef, mats, hf,
    cc_ref, ce_ref, tv, sv, mv, maps_ref, off_ref, table_ref, sun_ref, mix_ref, small_sem, load_sem, store_sem,
    halo_send, halo_recv, cour_send, cour_recv, mix_send, mix_recv, fwd_send, fwd_recv, ret_send, ret_recv,
):
    levels, cols, quarter, lanes, tiles, trc, substeps, entries = dims
    me_tile = lax.axis_index("tile")
    me = lax.axis_index("trc")
    after = lax.rem(me_tile + 1, tiles)
    before = lax.rem(me_tile + tiles - 1, tiles)

    first = pltpu.make_async_copy(cc_hbm, cc_ref, small_sem.at[0])
    first.start()
    loads = []
    for r in range(levels * cols):
        load = pltpu.make_async_copy(x_hbm.at[:, r, 0, :], xf.at[r], load_sem.at[r])
        load.start()
        loads.append(load)

    smalls = []
    for i, (source, target) in enumerate(
        ((mix_hbm, mv), (ce_hbm, ce_ref), (off_hbm, off_ref), (sun_hbm, sv), (table_hbm, tv), (maps_hbm, maps_ref))
    ):
        load = pltpu.make_async_copy(source, target, small_sem.at[i + 1])
        load.start()
        smalls.append(load)

    barrier = pltpu.get_barrier_semaphore()
    for other in (after, before):
        pl.semaphore_signal(barrier, inc=1, device_id={"tile": other, "trc": me}, device_id_type=MESH)
    for d in range(1, trc):
        pl.semaphore_signal(
            barrier, inc=1, device_id={"tile": me_tile, "trc": lax.rem(me + d, trc)}, device_id_type=MESH
        )
    first.wait()
    cs[...] = jnp.zeros_like(cs)
    for g in range(levels):
        cs[g : g + 1, :] = cc_ref[g * cols : g * cols + 1, :]
    pl.semaphore_wait(barrier, 2 + trc - 1)

    cour = pltpu.make_async_remote_copy(
        src_ref=cs, dst_ref=cr, send_sem=cour_send, recv_sem=cour_recv,
        device_id={"tile": before, "trc": me}, device_id_type=MESH,
    )
    cour.start()

    halos = []
    for g in range(levels):
        for c in range(cols):
            loads[g * cols + c].wait()
            xb[g, c] = xf[g * cols + c].astype(bf16)
        pair = []
        for way, (other, first, dst) in enumerate(((after, cols - WIDTH, hb), (before, 0, ha))):
            copy = pltpu.make_async_remote_copy(
                src_ref=xb.at[g, pl.ds(first, WIDTH)], dst_ref=dst.at[g],
                send_sem=halo_send.at[way, g], recv_sem=halo_recv.at[way, g],
                device_id={"tile": other, "trc": me}, device_id_type=MESH,
            )
            copy.start()
            pair.append(copy)
        halos.append(pair)
    for load in smalls:
        load.wait()
    mix_ref[...] = jnp.zeros_like(mix_ref)
    mix_ref[0 : levels - 1, :] = jnp.concatenate([mv[:, c, :] for c in range(cols)], axis=1)
    table_ref[...] = jnp.concatenate([tv[:, c, :] for c in range(cols)], axis=1)
    sun_ref[...] = jnp.concatenate([sv[c : c + 1, :] for c in range(cols)], axis=1)
    mixes = []
    for d in range(1, trc):
        copy = pltpu.make_async_remote_copy(
            src_ref=mix_ref, dst_ref=mg.at[me], send_sem=mix_send.at[d - 1], recv_sem=mix_recv.at[d - 1],
            device_id={"tile": me_tile, "trc": lax.rem(me + d, trc)}, device_id_type=MESH,
        )
        copy.start()
        mixes.append(copy)
    mg[me] = mix_ref[...]

    lane = lax.broadcasted_iota(jnp.int32, (CHUNK, lanes), 1)
    lane_block = lane // (lanes // trc)
    u_edge = ce_ref[...]
    row_lane = lax.broadcasted_iota(jnp.int32, u_edge.shape, 1)
    u_edge = jnp.where(row_lane == 0, 0.0, u_edge)
    wa, wb, wc = flux_weights(u_edge)
    wx[0], wx[1], wx[2], wx[3] = wa, wb, wc, u_edge
    chunks = quarter // CHUNK

    def edge_row(r, _):
        a_w = wx[0, pl.ds(r, 1), :]
        b_w = wx[1, pl.ds(r, 1), :]
        c_w = wx[2, pl.ds(r, 1), :]
        up = jnp.broadcast_to(wx[3, pl.ds(r, 1), :], (CHUNK, lanes)) > 0.0
        for i in range(chunks):
            cell = xf[r, pl.ds(i * CHUNK, CHUNK), :]
            m1 = jnp.where(lane < 1, cell, pltpu.roll(cell, 1, 1))
            m2 = jnp.where(lane < 2, m1, pltpu.roll(cell, 2, 1))
            m3 = jnp.where(lane < 3, m2, pltpu.roll(cell, 3, 1))
            p1 = jnp.where(lane == lanes - 1, cell, pltpu.roll(cell, lanes - 1, 1))
            p2 = jnp.where(lane >= lanes - 2, p1, pltpu.roll(cell, lanes - 2, 1))
            near = edge_value(m2, m1, cell, p1)
            far = edge_value(
                jnp.where(up, m3, m1), jnp.where(up, m2, cell), jnp.where(up, m1, p1), jnp.where(up, cell, p2)
            )
            flux = a_w * near + b_w * far + c_w * jnp.where(up, m1, cell)
            yb[r, pl.ds(i * CHUNK, CHUNK), :] = cell + (flux - pltpu.roll(flux, lanes - 1, 1))
        return 0

    lax.fori_loop(0, levels * cols, edge_row, 0, unroll=4)

    for e in range(entries):
        picked = lax.broadcasted_iota(jnp.int32, (entries, lanes), 0) == e
        offb[e] = lax.dot_general(
            off_ref[...], jnp.where(picked, 1.0, 0.0), (((0,), (0,)), ((), ())),
            precision=lax.Precision.HIGHEST, preferred_element_type=f32,
        )
    src = lax.broadcasted_iota(jnp.int32, (lanes, lanes), 0)
    dst = lax.broadcasted_iota(jnp.int32, (lanes, lanes), 1)
    for side in range(2):
        target = jnp.where(flag_ref[0, side] > 0, lanes - 1 - src, src)
        mats[side] = jnp.where(target == dst, 1.0, 0.0)

    cour.wait()
    u_after = jnp.dot(cr[...], mats[1], precision=lax.Precision.HIGHEST, preferred_element_type=f32)
    for g in range(levels):
        coef[3, g] = jnp.zeros(coef.shape[2:], f32)
        coef[3, g, 0:cols, :] = cc_ref[g * cols : (g + 1) * cols, :]
        coef[3, g, cols : cols + 1, :] = u_after[g : g + 1, :]
    wa, wb, wc = flux_weights(coef[3])
    coef[0], coef[1], coef[2] = wa, wb, wc
    rev = [mats[side].astype(bf16) for side in range(2)]

    def cycle_level(g):
        for copy in halos[g]:
            copy.wait_recv()
        for side, halo in enumerate((hb, ha)):
            turned = jnp.dot(halo[g].reshape(WIDTH * quarter, lanes), rev[side], preferred_element_type=f32)
            hf[side] = turned.reshape(WIDTH, quarter, lanes)
        ups = [jnp.broadcast_to(coef[3, g, f : f + 1, :], (CHUNK, lanes)) > 0.0 for f in range(cols + 1)]

        def chunk(i, _):
            rows = pl.ds(pl.multiple_of(i * CHUNK, CHUNK), CHUNK)
            cells = [hf[0, k, rows, :] for k in range(WIDTH)]
            cells += [xf[g * cols + c, rows, :] for c in range(cols)]
            cells += [hf[1, k, rows, :] for k in range(WIDTH)]
            edges = [edge_value(*cells[k : k + 4]) for k in range(cols + 3)]
            fluxes = []
            for f in range(cols + 1):
                far = jnp.where(ups[f], edges[f], edges[f + 2])
                q = jnp.where(ups[f], cells[f + 2], cells[f + 3])
                fluxes.append(
                    coef[0, g, f : f + 1, :] * edges[f + 1]
                    + coef[1, g, f : f + 1, :] * far
                    + coef[2, g, f : f + 1, :] * q
                )
            moved = [yb[g * cols + c, rows, :] + (fluxes[c] - fluxes[c + 1]) for c in range(cols)]
            moved = block_transpose(moved, lane_block)
            for p in range(trc):
                sb[g, p, rows, :] = moved[p].astype(bf16)
            return 0

        lax.fori_loop(0, chunks, chunk, 0, unroll=chunks)
        sends = []
        for d in range(1, trc):
            peer = lax.rem(me + d, trc)
            copy = pltpu.make_async_remote_copy(
                src_ref=sb.at[g, peer], dst_ref=cb.at[g, me],
                send_sem=fwd_send.at[d - 1, g], recv_sem=fwd_recv.at[d - 1, g],
                device_id={"tile": me_tile, "trc": peer}, device_id_type=MESH,
            )
            copy.start()
            sends.append(copy)
        cb[g, me] = sb[g, me]
        return sends

    species = quarter * trc
    sun = jnp.broadcast_to(sun_ref[...], (species, lanes)) > 0

    def chem_levels(group):
        for g in group:
            for copy in sends[g]:
                copy.wait_recv()
        conc = [cb[g].reshape(species, lanes) for g in group]
        states = conc
        for s in range(substeps):
            product = jnp.dot(maps_ref[...], jnp.concatenate(states, axis=1), preferred_element_type=f32)
            results = []
            for i, g in enumerate(group):
                row = s * levels + g
                entry = jnp.broadcast_to(table_ref[row : row + 1, :], (species, lanes))
                part = product[:, i * lanes : (i + 1) * lanes]
                result = part[:species] + offb[0]
                for e in range(1, entries):
                    result = jnp.where(entry == e, part[e * species : (e + 1) * species] + offb[e], result)
                results.append(jnp.maximum(result, 0.0))
            states = [result.astype(bf16) for result in results]
        copies = []
        for i, g in enumerate(group):
            chem = jnp.where(sun, results[i], conc[i].astype(f32)).astype(bf16)
            rs[g] = chem.reshape(trc, quarter, lanes)
            for d in range(1, trc):
                peer = lax.rem(me + d, trc)
                copy = pltpu.make_async_remote_copy(
                    src_ref=rs.at[g, peer], dst_ref=back.at[g, me],
                    send_sem=ret_send.at[d - 1, g], recv_sem=ret_recv.at[d - 1, g],
                    device_id={"tile": me_tile, "trc": peer}, device_id_type=MESH,
                )
                copy.start()
                copies.append(copy)
            back[g, me] = rs[g, me]
        return copies

    sends = [cycle_level(g) for g in range(levels)]
    returns = [chem_levels(range(g, min(g + 2, levels))) for g in range(0, levels, 2)]

    for copy in mixes:
        copy.wait()
    small_block = lax.broadcasted_iota(jnp.int32, mg.shape[1:], 1) // (lanes // trc)
    mixing = block_transpose([mg[q] for q in range(trc)], small_block)
    inverse, below, ratio = [], [], []
    for c in range(cols):
        k = [mixing[c][l : l + 1, :] for l in range(levels - 1)]
        inv_c, rat_c = [], []
        for l in range(levels):
            k_low = k[l - 1] if l > 0 else None
            k_high = k[l] if l < levels - 1 else None
            pivot = 1.0
            if k_low is not None:
                pivot = pivot + k_low - k_low * rat_c[-1]
            if k_high is not None:
                pivot = pivot + k_high
            inv = 1.0 / pivot
            inv_c.append(inv)
            rat_c.append(k_high * inv if k_high is not None else None)
        inverse.append(inv_c)
        ratio.append(rat_c)
        below.append(k)

    for pair in returns:
        for copy in pair:
            copy.wait_recv()

    def solve_chunk(i, _):
        rows = pl.ds(pl.multiple_of(i * CHUNK, CHUNK), CHUNK)
        chem = []
        for g in range(levels):
            chem.append(block_transpose([back[g, q, rows, :].astype(f32) for q in range(trc)], lane_block))
        for c in range(cols):
            solved = []
            for l in range(levels):
                value = chem[l][c]
                if l > 0:
                    value = value + below[c][l - 1] * solved[-1]
                solved.append(value * inverse[c][l])
            current = solved[-1]
            xf[(levels - 1) * cols + c, rows, :] = current
            for l in range(levels - 2, -1, -1):
                current = solved[l] + ratio[c][l] * current
                xf[l * cols + c, rows, :] = current
        return 0

    stores = []
    half = chunks // 2
    for part, (low, high) in enumerate(((0, half), (half, chunks))):
        lax.fori_loop(low, high, solve_chunk, 0, unroll=2)
        rows = pl.ds(low * CHUNK, (high - low) * CHUNK)
        for r in range(levels * cols):
            store = pltpu.make_async_copy(xf.at[r, rows], out_hbm.at[rows, r, 0, :], store_sem.at[part, r])
            store.start()
            stores.append(store)
    for group in halos + sends + returns:
        for copy in group:
            copy.wait_send()
    for store in stores:
        store.wait()


def shards(
    tiles, trc,
    tracers, courant_cycle, courant_edge, seam_flags, sunlit, table_entry, linear_maps, offsets, mixing,
):
    quarter, levels, cols, lanes = tracers.shape
    substeps = table_entry.shape[0]
    entries, species, _ = linear_maps.shape
    rows = levels * cols
    dims = (levels, cols, quarter, lanes, tiles, trc, substeps, entries)
    hbm = pl.BlockSpec(memory_space=pl.ANY)
    smem = pl.BlockSpec(memory_space=pltpu.SMEM)
    dma = pltpu.SemaphoreType.DMA
    out = pl.pallas_call(
        functools.partial(kernel, dims),
        out_shape=jax.ShapeDtypeStruct((quarter, rows, 1, lanes), f32),
        in_specs=[hbm, hbm, hbm, smem, hbm, hbm, hbm, hbm, hbm],
        out_specs=hbm,
        scratch_shapes=[
            pltpu.VMEM((rows, quarter, lanes), f32),
            pltpu.VMEM((rows, quarter, lanes), f32),
            pltpu.VMEM((levels, cols, quarter, lanes), bf16),
            pltpu.VMEM((levels, WIDTH, quarter, lanes), bf16),
            pltpu.VMEM((levels, WIDTH, quarter, lanes), bf16),
            pltpu.VMEM((8, lanes), f32),
            pltpu.VMEM((8, lanes), f32),
            pltpu.VMEM((4, rows, lanes), f32),
            pltpu.VMEM((levels, trc, quarter, lanes), bf16),
            pltpu.VMEM((levels, trc, quarter, lanes), bf16),
            pltpu.VMEM((levels, trc, quarter, lanes), bf16),
            pltpu.VMEM((levels, trc, quarter, lanes), bf16),
            pltpu.VMEM((trc, 8, lanes), f32),
            pltpu.VMEM((entries, species, lanes), f32),
            pltpu.VMEM((4, levels, 8, lanes), f32),
            pltpu.VMEM((2, lanes, lanes), f32),
            pltpu.VMEM((2, WIDTH, quarter, lanes), f32),
            pltpu.VMEM((rows, lanes), f32),
            pltpu.VMEM((rows, lanes), f32),
            pltpu.VMEM((substeps * levels, cols, lanes // trc), jnp.int32),
            pltpu.VMEM((cols, lanes // trc), jnp.int32),
            pltpu.VMEM((levels - 1, cols, lanes // trc), f32),
            pltpu.VMEM((entries * species, species), bf16),
            pltpu.VMEM((entries, species), f32),
            pltpu.VMEM((substeps * levels, lanes), jnp.int32),
            pltpu.VMEM((1, lanes), jnp.int32),
            pltpu.VMEM((8, lanes), f32),
            dma((7,)),
            dma((rows,)),
            dma((2, rows)),
            dma((2, levels)),
            dma((2, levels)),
            dma,
            dma,
            dma((trc - 1,)),
            dma((trc - 1,)),
            dma((trc - 1, levels)),
            dma((trc - 1, levels)),
            dma((trc - 1, levels)),
            dma((trc - 1, levels)),
        ],
        compiler_params=pltpu.CompilerParams(
            collective_id=0, has_side_effects=True, vmem_limit_bytes=60 * 1024 * 1024
        ),
    )(
        tracers.reshape(quarter, rows, 1, lanes),
        courant_cycle.reshape(rows, lanes),
        courant_edge.reshape(rows, lanes),
        seam_flags,
        table_entry.reshape(substeps * levels, cols, lanes // trc),
        sunlit,
        mixing,
        linear_maps.reshape(entries * species, species),
        offsets,
    )
    return out.reshape(tracers.shape)


def solution(mesh):
    placed = (
        P("trc", None, "tile", None),
        P(None, "tile", None),
        P(None, "tile", None),
        P("tile", None),
        P("tile", "trc"),
        P(None, None, "tile", "trc"),
        P(),
        P(),
        P(None, "tile", "trc"),
    )
    return jax.shard_map(
        functools.partial(shards, mesh.shape["tile"], mesh.shape["trc"]),
        mesh=mesh, in_specs=placed, out_specs=P("trc", None, "tile", None), check_vma=False,
    )
```
